128 devices in a mesh: aux: 4 (over z_lo, core), bas: 32 (over x, z_hi, y).
Axes of the slice: x: 4, y: 4, z: 4 (z_hi: 2, z_lo: 2; z = z_hi * 2 + z_lo), core: 2. Of those that a mesh axis runs over, the one named last changes fastest.
Arguments:
- slabs: bfloat16 [512, 8, 12288], P('aux', None, 'bas'), may hold values from -0.09375 to 0.09375
Outputs:
- exchange: float32 [12288, 12288], P('aux', 'bas')
The draws below stay inside these ranges and needn't reach their ends.
All inputs are finite; a program needn't handle non-finite values.
Results may differ from the reference program's by a relative error of at most 0.0003.
Values may be sent and summed in bfloat16 or wider, within the bound.
A program may use at most 128 MiB of HBM per device.

```python
import jax
import jax.numpy as jnp

OCC = 8
NAUX = 512
NBAS = 12288


def spiked(array, rng, source, target, blocks, factor):
    owner, partner = [(jnp.arange(array.shape[position]) // (array.shape[position] // blocks)).reshape([-1 if axis == position else 1 for axis in range(array.ndim)]) for position in (source, target)]
    chosen = jax.random.permutation(rng, blocks)[partner]
    strong = (owner == chosen) | (owner == (partner + blocks // 2) % blocks)
    return jnp.where(strong, factor * array, array)


def block_levels(rng, shape, pieces, low, largest):
    factor_of, own = 1.0, jax.random.fold_in(rng, 6)
    for dim, blocks in pieces:
        steps = jnp.exp(jax.random.uniform(jax.random.fold_in(own, dim), (blocks,), jnp.float32, low / len(pieces), largest / len(pieces)))
        factor_of = factor_of * jnp.repeat(steps, shape[dim] // blocks).reshape([-1 if axis == dim else 1 for axis in range(len(shape))])
    return factor_of


def bell_draw_with(rng, dims, deviation, reach, pieces, heavy, kind=jnp.bfloat16):
    values = deviation * jax.random.normal(rng, dims, jnp.float32)
    if pieces:
        values = values * block_levels(rng, dims, pieces, -0.22, 0.18)
    return jnp.clip(spiked(values, jax.random.fold_in(rng, 3), *heavy), -reach, reach).astype(kind)


def setup_inputs(seed: int = 0) -> dict:
    arg_keys = jax.random.split(jax.random.key(seed), 2)
    return {
        "slabs": bell_draw_with(arg_keys[0], (NAUX, OCC, NBAS), (1.0 / (NAUX * OCC) ** 0.5), 0.09375, ((0, 4), (2, 32)), (0, 2, 32, 2.75)),
    }


def reference(slabs):
    flat = slabs.reshape(NAUX * OCC, NBAS)
    return jnp.dot(flat.T, flat, preferred_element_type=jnp.float32)
```

```python
import functools

import jax
import jax.numpy as jnp
from jax import lax
from jax.experimental import pallas as pl
from jax.experimental.pallas import tpu as pltpu
from jax.sharding import PartitionSpec as P

MESH = pl.DeviceIdType.MESH
BLOCK, HALF, QUARTER, DEPTH = 384, 192, 96, 1024


def encode(tile):
    largest = jnp.max(jnp.abs(tile), axis=(0, 1), keepdims=True)
    largest = jnp.maximum(largest, 1e-30)
    t = tile * (16384.0 / largest)
    t2 = t * t
    code = (t2 * t2) * (t2 * t) * jnp.abs(t)
    return code.astype(jnp.bfloat16), largest * (1.0 / 16384.0)


def decode(code, factor):
    code = code.astype(jnp.float32)
    root = jnp.sqrt(jnp.sqrt(jnp.sqrt(jnp.abs(code))))
    return jnp.where(code < 0, -root, root) * factor


def kernel(bt, land, factors, cb, rb, psend, precv, pown, enc, fac, ss, rs, ls, pss, prs, rss, rrs, fss, frs, own_sem):
    aux, bas = lax.axis_index("aux"), lax.axis_index("bas")
    zl, h = aux // 2, lax.rem(aux, 2)
    x, zh, y = bas // 8, lax.rem(bas // 4, 2), lax.rem(bas, 4)
    zb = lax.rem(zl + zh, 2)

    def device(x=x, y=y, zh=zh, zl=zl, h=h):
        return (zl * 2 + h, x * 8 + zh * 4 + y)

    def ring(v, step):
        return lax.rem(v + step + 4, 4)

    right, left = {"y": ring(y, 1)}, {"y": ring(y, -1)}
    front, back = {"x": ring(x, 1)}, {"x": ring(x, -1)}
    a_dev = device(zl=1 - zl)
    b_dev = device(zl=1 - zl, zh=1 - zh)
    core_dev = device(h=1 - h)

    barrier = pltpu.get_barrier_semaphore()
    greeted = [device(**d) for d in (right, left, front, back)] + [a_dev, b_dev, core_dev]
    greeted += [device(y=ring(y, 2)), device(y=ring(y, 1), zl=1 - zl), device(y=ring(y, 2), zl=1 - zl), device(y=ring(y, 3), zl=1 - zl)]
    for d in greeted:
        pl.semaphore_signal(barrier, 1, device_id=d, device_id_type=MESH)
    pl.semaphore_wait(barrier, len(greeted))

    count = [0]
    started = []

    def send(src, dst, to):
        n = count[0]
        count[0] += 1
        copy = pltpu.make_async_remote_copy(src, dst, ss.at[n], rs.at[n], device_id=to, device_id_type=MESH)
        copy.start()
        started.append(copy)
        return copy

    def local(src, dst, n):
        copy = pltpu.make_async_copy(src, dst, ls.at[n])
        copy.start()
        return copy

    def both(src, dst, plus, minus):
        return send(src, dst, device(**plus)), send(src, dst, device(**minus))

    def forward(slots, where, plus, minus):
        lo, hi = pl.ds(0, QUARTER), pl.ds(QUARTER, QUARTER)
        a = slots(ring(where, -1)).at[lo]
        b = slots(ring(where, 1)).at[hi]
        return send(a, a, device(**plus)), send(b, b, device(**minus))

    other = 1 - zb
    a1 = send(bt.at[other], cb.at[y, zl, other], a_dev)
    b1 = send(bt.at[zb], rb.at[x, zl, zh], b_dev)
    n1 = both(bt.at[zb], cb.at[y, zl, zb], right, left)
    q0 = both(bt.at[zb], rb.at[x, zl, zh], front, back)
    a2 = [send(bt.at[zb], cb.at[y, zl, zb], a_dev)]
    l0 = local(bt, cb.at[y, zl], 0)
    l1 = local(bt.at[zb], rb.at[x, zl, zh], 1)
    l0.wait()
    l1.wait()

    def n1_slot(v):
        return cb.at[v, zl, zb]

    def n0_slot(v):
        return cb.at[v, zl, other]

    def p0_slot(v):
        return cb.at[v, 1 - zl, zb]

    def q0_slot(v):
        return rb.at[v, zl, zh]

    def q1_slot(v):
        return rb.at[v, 1 - zl, 1 - zh]

    def q2_slot(v):
        return rb.at[v, 1 - zl, zh]

    a1.wait_recv()
    b1.wait_recv()
    l2 = local(p0_slot(y), q2_slot(x), 2)
    p0 = both(p0_slot(y), p0_slot(y), right, left)
    q2 = both(p0_slot(y), q2_slot(x), front, back)
    b2 = [send(p0_slot(y), q2_slot(x), b_dev)]
    for c in n1 + q0:
        c.wait_recv()
    n1f = forward(n1_slot, y, right, left)
    q0f = forward(q0_slot, x, front, back)
    a2.append(send(n1_slot(ring(y, -1)), n1_slot(ring(y, -1)), a_dev))
    a2.append(send(n1_slot(ring(y, 1)), n1_slot(ring(y, 1)), a_dev))
    n0 = both(bt.at[other], n0_slot(y), right, left)
    q1 = both(q1_slot(x), q1_slot(x), front, back)
    l2.wait()
    for c in p0 + q2:
        c.wait_recv()
    p0f = forward(p0_slot, y, right, left)
    q2f = forward(q2_slot, x, front, back)
    b2.append(send(q2_slot(ring(x, -1)), q2_slot(ring(x, -1)), b_dev))
    b2.append(send(q2_slot(ring(x, 1)), q2_slot(ring(x, 1)), b_dev))
    for c in n1f:
        c.wait_recv()
    a2.append(send(n1_slot(ring(y, 2)), n1_slot(ring(y, 2)), a_dev))
    for c in n0 + q1:
        c.wait_recv()
    n0f = forward(n0_slot, y, right, left)
    q1f = forward(q1_slot, x, front, back)
    for c in q2f:
        c.wait_recv()
    b2.append(send(q2_slot(ring(x, 2)), q2_slot(ring(x, 2)), b_dev))

    def product(xs, ys):
        total = None
        for k in range(2):
            part = lax.dot_general(
                rb[xs, k].reshape(BLOCK, DEPTH), cb[ys, k].reshape(BLOCK, DEPTH), (((1,), (1,)), ((), ())), preferred_element_type=jnp.float32
            )
            total = part if total is None else total + part
        return total

    exchanged = []

    def task(j, i, ys):
        psend[j] = product(2 * i + 1 - h, ys)
        copy = pltpu.make_async_remote_copy(psend.at[j], precv.at[j], pss.at[j], prs.at[j], device_id=core_dev, device_id_type=MESH)
        copy.start()
        exchanged.append(copy)
        pown[j] = product(2 * i + h, ys)

    finals = []

    def finish(j, i, step):
        ys = ring(y, step)
        exchanged[j].wait_recv()
        code, factor = encode(pown[j] + precv[j])
        enc[j] = code.reshape(2, HALF, BLOCK)
        fac[j] = jnp.broadcast_to(factor, (8, 128))
        owner = device(y=ys, zl=i)
        slot = y * 2 + zb
        flip = lax.rem(i + zl, 2)
        n = step * 2 + flip
        copy = pltpu.make_async_remote_copy(enc.at[j], land.at[:, slot], rss.at[n], rrs.at[n], device_id=owner, device_id_type=MESH)
        scale = pltpu.make_async_remote_copy(fac.at[j], factors.at[slot], fss.at[n], frs.at[n], device_id=owner, device_id_type=MESH)
        if step:
            copy.start()
            scale.start()
        else:

            @pl.when(flip == 1)
            def _():
                copy.start()
                scale.start()

            @pl.when(flip == 0)
            def _():
                mine = pltpu.make_async_copy(enc.at[j], land.at[:, slot], own_sem.at[0])
                mine.start()
                scale_mine = pltpu.make_async_copy(fac.at[j], factors.at[slot], own_sem.at[1])
                scale_mine.start()
                mine.wait()
                scale_mine.wait()

    i0 = x // 2
    order = [(0, 0), (0, 3), (0, 1), (1, 0), (1, 3), (1, 1), (0, 2), (1, 2)]
    for c in list(a2[:1]) + list(b2[:1]):
        c.wait_recv()
    for c in list(a2[1:3]) + list(b2[1:3]):
        c.wait_recv()
    for c in q0f + p0f + n0f + q1f:
        c.wait_recv()
    a2[3].wait_recv()
    b2[3].wait_recv()
    for j, (flip_x, step) in enumerate(order):
        i = i0 if flip_x == 0 else 1 - i0
        task(j, i, ring(y, step))
        if j:
            fx, st = order[j - 1]
            finish(j - 1, i0 if fx == 0 else 1 - i0, st)
    fx, st = order[-1]
    finish(len(order) - 1, i0 if fx == 0 else 1 - i0, st)

    for n in range(1, 8):
        copy = pltpu.make_async_remote_copy(enc.at[0], land.at[:, 0], rss.at[n], rrs.at[n], device_id=a_dev, device_id_type=MESH)
        scale = pltpu.make_async_remote_copy(fac.at[0], factors.at[0], fss.at[n], frs.at[n], device_id=a_dev, device_id_type=MESH)
        copy.wait()
        scale.wait()
    for c in exchanged + started:
        c.wait_send()


def shards(slabs):
    flat = slabs.reshape(-1, BLOCK)
    blocks = flat.T.reshape(2, HALF, DEPTH)
    anywhere = pl.BlockSpec(memory_space=pl.ANY)
    dma = pltpu.SemaphoreType.DMA
    copies = 40
    land, factors = pl.pallas_call(
        kernel,
        out_shape=(
            jax.ShapeDtypeStruct((2, 8, HALF, BLOCK), jnp.bfloat16),
            jax.ShapeDtypeStruct((8, 8, 128), jnp.float32),
        ),
        in_specs=[anywhere],
        out_specs=(anywhere, anywhere),
        scratch_shapes=[
            pltpu.VMEM((4, 2, 2, HALF, DEPTH), jnp.bfloat16),
            pltpu.VMEM((4, 2, 2, HALF, DEPTH), jnp.bfloat16),
            pltpu.VMEM((8, BLOCK, BLOCK), jnp.float32),
            pltpu.VMEM((8, BLOCK, BLOCK), jnp.float32),
            pltpu.VMEM((8, BLOCK, BLOCK), jnp.float32),
            pltpu.VMEM((8, 2, HALF, BLOCK), jnp.bfloat16),
            pltpu.VMEM((8, 8, 128), jnp.float32),
            dma((copies,)), dma((copies,)), dma((3,)),
            dma((8,)), dma((8,)), dma((8,)), dma((8,)), dma((8,)), dma((8,)), dma((2,)),
        ],
        compiler_params=pltpu.CompilerParams(collective_id=0, has_side_effects=True, vmem_limit_bytes=50 * 2**20),
        cost_estimate=pl.CostEstimate(flops=2 * 1536 * 1536 * 2048, bytes_accessed=4 * 2**20, transcendentals=0),
    )(blocks)
    factor = factors[:, 0, 0].reshape(1, 8, 1, 1)
    return decode(land, factor).reshape(8 * BLOCK, BLOCK)


def solution(mesh):
    placed = (P("aux", None, "bas"),)
    return jax.shard_map(
        shards, mesh=mesh, in_specs=placed, out_specs=P("aux", "bas"), check_vma=False
    )
```

```python
import jax
import jax.numpy as jnp
from jax import lax
from jax.experimental import pallas as pl
from jax.experimental.pallas import tpu as pltpu
from jax.sharding import PartitionSpec as P

MESH = pl.DeviceIdType.MESH
BLOCK, HALF, QUARTER, DEPTH = 384, 192, 96, 1024
TOP = 208.0


def encode(tile):
    largest = jnp.max(jnp.abs(tile), axis=1, keepdims=True)
    largest = jnp.maximum(largest, 1e-30)
    t = tile * (TOP / largest)
    t2 = t * t
    t4 = t2 * t2
    code = (t4 * t4) * (t4 * t2) * (t * jnp.abs(t))
    return code.astype(jnp.bfloat16), largest * (1.0 / TOP)


def decode(code, factor):
    code = code.astype(jnp.float32)
    root = jnp.exp2(jnp.log2(jnp.abs(code)) * (1.0 / 16.0))
    return jnp.where(code < 0, -root, root) * factor


def place():
    aux, bas = lax.axis_index("aux"), lax.axis_index("bas")
    return aux // 2, lax.rem(aux, 2), bas // 8, lax.rem(bas // 4, 2), lax.rem(bas, 4)


def ring(v, step):
    return lax.rem(v + step + 4, 4)


def is_turned(dx, dy):
    far_x, far_y = min(dx, 4 - dx), min(dy, 4 - dy)
    return far_x < far_y or far_x == far_y > 0


def kernel(bt, out, cb, rb, part, precv, enc, fac, land, factors, staged, ss, rs, ls, pss, prs, rss, rrs, fss, frs, os, outs):
    zl, h, x, zh, y = place()
    a = zl * 2 + h
    zb = lax.rem(zl + zh, 2)
    other = 1 - zb

    def device(x=x, y=y, zh=zh, zl=zl, h=h):
        return (zl * 2 + h, x * 8 + zh * 4 + y)

    right, left = {"y": ring(y, 1)}, {"y": ring(y, -1)}
    front, back = {"x": ring(x, 1)}, {"x": ring(x, -1)}
    a_dev = device(zl=1 - zl)
    b_dev = device(zl=1 - zl, zh=1 - zh)
    core_dev = device(h=1 - h)

    barrier = pltpu.get_barrier_semaphore()
    greeted = [device(**front), device(**back), b_dev, core_dev, a_dev]
    greeted += [device(y=ring(y, step), zl=z) for step in (1, 2, 3) for z in (zl, 1 - zl)]
    for d in greeted:
        pl.semaphore_signal(barrier, 1, device_id=d, device_id_type=MESH)
    alone = a == x
    for zh1 in range(2):
        for zl1 in range(2):
            same = jnp.logical_and(alone, jnp.logical_and(zh == zh1, zl == zl1))

            @pl.when(jnp.logical_not(same))
            def _():
                pl.semaphore_signal(barrier, 1, device_id=device(x=a, zh=zh1, zl=zl1, h=lax.rem(x, 2)), device_id_type=MESH)

    pl.semaphore_wait(barrier, len(greeted) + 4 - alone.astype(jnp.int32))

    started = []

    def send(src, dst, to):
        n = len(started)
        copy = pltpu.make_async_remote_copy(src, dst, ss.at[n], rs.at[n], device_id=to, device_id_type=MESH)
        copy.start()
        started.append(copy)
        return copy

    def local(src, dst, n):
        copy = pltpu.make_async_copy(src, dst, ls.at[n])
        copy.start()
        return copy

    def both(src, dst, plus, minus):
        return [send(src, dst, device(**plus)), send(src, dst, device(**minus))]

    def forward(slots, where, plus, minus, rows=HALF):
        lo, hi = pl.ds(0, rows // 2), pl.ds(rows // 2, rows // 2)
        one = slots(ring(where, -1)).at[lo]
        two = slots(ring(where, 1)).at[hi]
        return [send(one, one, device(**plus)), send(two, two, device(**minus))]

    def n1_slot(v):
        return cb.at[v, zl, zb]

    def n0_slot(v):
        return cb.at[v, zl, other]

    def p0_slot(v):
        return cb.at[v, 1 - zl, zb]

    def p1_slot(v):
        return cb.at[v, 1 - zl, other, pl.ds(0, QUARTER)]

    def a2_slot(v):
        return cb.at[v, zl, zb, pl.ds(QUARTER, QUARTER)]

    def q0_slot(v):
        return rb.at[v, zl, zh]

    def q1_slot(v):
        return rb.at[v, 1 - zl, 1 - zh]

    def q2_slot(v):
        return rb.at[v, 1 - zl, zh]

    def arrive(*copies):
        for group in copies:
            for c in group:
                c.wait_recv()

    def product(xs, ys):
        total = None
        for k in range(2):
            term = lax.dot_general(
                rb[xs, k].reshape(BLOCK, DEPTH), cb[ys, k].reshape(BLOCK, DEPTH), (((1,), (1,)), ((), ())), preferred_element_type=jnp.float32
            )
            total = term if total is None else total + term
        return total

    tasks, ends = [], []

    def task(dx, dy):
        j = len(tasks)
        xs = ring(x, dx)
        keep = lax.rem(xs, 2) == h
        ys = ring(y, dy)
        spot = (xs // 2) * 4 + ys
        part[j] = product(xs, ys)
        copy = pltpu.make_async_remote_copy(part.at[j], precv.at[spot], pss.at[j], prs.at[spot], device_id=core_dev, device_id_type=MESH)
        pl.when(jnp.logical_not(keep))(copy.start)
        ends.append((jnp.logical_not(keep), [copy.wait_send]))
        tasks.append((dx, dy, xs, ys, keep, spot, copy))
        if j:
            finish(j - 1)

    def finish(j):
        dx, dy, xs, ys, keep, spot, exchanged = tasks[j]

        def deliver(zh1, owner, slot_zh, slot_y, mine):
            n = j * 2 + zh1
            piece = (slot_zh * 4 + slot_y) * 2 + zb
            src, src_factor = enc.at[spot, zh1], fac.at[spot, zh1]
            dst, dst_factor = land.at[slot_zh, slot_y, zb], factors.at[slot_zh, slot_y, zb]
            away = [
                pltpu.make_async_remote_copy(src, dst, rss.at[n], rrs.at[piece], device_id=owner, device_id_type=MESH),
                pltpu.make_async_remote_copy(src_factor, dst_factor, fss.at[n], frs.at[piece], device_id=owner, device_id_type=MESH),
            ]
            home = []
            if mine is not None:
                home = [pltpu.make_async_copy(src, dst, os.at[0]), pltpu.make_async_copy(src_factor, dst_factor, os.at[1])]
            ends.append((keep if mine is None else jnp.logical_and(keep, jnp.logical_not(mine)), [c.wait_send for c in away]))
            return away, home, mine

        pieces = []
        for zh1 in range(2):
            if is_turned(dx, dy):
                mine = jnp.logical_and(alone, zh == zh1) if dx == 0 else None
                pieces.append(deliver(zh1, device(x=xs, zh=zh1, zl=x // 2, h=lax.rem(x, 2)), zh, ys, mine))
            else:
                mine = xs == a if dy == 0 else None
                pieces.append(deliver(zh1, device(y=ys, zl=xs // 2), zh1, y, mine))

        @pl.when(keep)
        def _():
            exchanged.wait_recv()
            code, factor = encode((part[j] + precv[spot]).reshape(2, HALF, BLOCK))
            enc[spot] = code
            fac[spot] = jnp.broadcast_to(factor, (2, 8, BLOCK))
            for away, home, mine in pieces:
                if mine is None:
                    for c in away:
                        c.start()
                    continue

                @pl.when(jnp.logical_not(mine))
                def _():
                    for c in away:
                        c.start()

                @pl.when(mine)
                def _():
                    for c in home:
                        c.start()
                    for c in home:
                        c.wait()

    a1 = [send(bt.at[other], cb.at[y, zl, other], a_dev)]
    b1 = [send(bt.at[zb], rb.at[x, zl, zh], b_dev)]
    n1 = both(bt.at[zb], cb.at[y, zl, zb], right, left)
    q0 = both(bt.at[zb], rb.at[x, zl, zh], front, back)
    a1b = [send(bt.at[zb, pl.ds(0, QUARTER)], cb.at[y, zl, zb, pl.ds(0, QUARTER)], a_dev)]
    a2 = {0: [send(bt.at[zb, pl.ds(QUARTER, QUARTER)], a2_slot(y), a_dev)]}
    b2 = {}
    l0 = local(bt, cb.at[y, zl], 0)
    l1 = local(bt.at[zb], rb.at[x, zl, zh], 1)

    arrive(a1)
    l2 = local(p0_slot(y), q2_slot(x), 2)
    p0 = both(p0_slot(y), p0_slot(y), right, left)
    q2 = both(p0_slot(y), q2_slot(x), front, back)
    b2[0] = [send(p0_slot(y), q2_slot(x), b_dev)]
    arrive(n1)
    n1f = forward(n1_slot, y, right, left)
    for step in (3, 1):
        a2[step] = [send(a2_slot(ring(y, step)), a2_slot(ring(y, step)), a_dev)]
    arrive(q0)
    q0f = forward(q0_slot, x, front, back)
    arrive(b1)
    q1 = both(q1_slot(x), q1_slot(x), front, back)
    arrive(a1b)
    p1 = both(p1_slot(y), p1_slot(y), right, left)
    n0 = both(bt.at[other], n0_slot(y), right, left)
    arrive(q2)
    q2f = forward(q2_slot, x, front, back)
    for step in (3, 1):
        b2[step] = [send(q2_slot(ring(x, step)), q2_slot(ring(x, step)), b_dev)]
    arrive(p0)
    p0f = forward(p0_slot, y, right, left)
    arrive(n1f)
    a2[2] = [send(a2_slot(ring(y, 2)), a2_slot(ring(y, 2)), a_dev)]
    l0.wait()
    l1.wait()
    l2.wait()
    arrive(a2[0], b2[0])
    task(0, 0)
    arrive(p1)
    p1f = forward(p1_slot, y, right, left, QUARTER)
    arrive(q2f)
    b2[2] = [send(q2_slot(ring(x, 2)), q2_slot(ring(x, 2)), b_dev)]
    arrive(q1)
    q1f = forward(q1_slot, x, front, back)
    arrive(n0)
    n0f = forward(n0_slot, y, right, left)
    arrive(b2[3])
    task(3, 0)
    arrive(a2[3])
    task(0, 3)
    task(3, 3)
    arrive(b2[1])
    task(1, 0)
    task(1, 3)
    arrive(a2[1])
    task(0, 1)
    task(3, 1)
    task(1, 1)
    arrive(q0f, q1f, b2[2])
    task(2, 0)
    task(2, 3)
    task(2, 1)
    arrive(p0f, n0f, p1f, a2[2])
    task(2, 2)
    task(3, 2)
    task(1, 2)
    task(0, 2)
    finish(15)

    def unpack(k, carry):
        q = k // 2
        slot_zh = lax.rem(k, 2)
        step = q + (q == 2).astype(jnp.int32) - (q == 3).astype(jnp.int32)
        slot_y = ring(y, step)
        for slot_zb in range(2):
            mine = jnp.logical_and(slot_zb == zb, jnp.logical_or(step == 0, jnp.logical_and(alone, slot_zh == zh)))
            piece = (slot_zh * 4 + slot_y) * 2 + slot_zb

            @pl.when(jnp.logical_not(mine))
            def _():
                dst, dst_factor = land.at[slot_zh, slot_y, slot_zb], factors.at[slot_zh, slot_y, slot_zb]
                pltpu.make_async_remote_copy(enc.at[0, 0], dst, rss.at[0], rrs.at[piece], device_id=a_dev, device_id_type=MESH).wait_recv()
                pltpu.make_async_remote_copy(fac.at[0, 0], dst_factor, fss.at[0], frs.at[piece], device_id=a_dev, device_id_type=MESH).wait_recv()

        values = decode(land[slot_zh, slot_y], factors[slot_zh, slot_y, :, :1]).reshape(BLOCK, BLOCK)
        dx, dy = ring(a, -x), lax.rem(4 - step, 4)
        far_x, far_y = jnp.minimum(dx, 4 - dx), jnp.minimum(dy, 4 - dy)
        turned = jnp.logical_or(far_x < far_y, jnp.logical_and(far_x == far_y, far_x > 0))

        @pl.when(turned)
        def _():
            staged[k] = values.T

        @pl.when(jnp.logical_not(turned))
        def _():
            staged[k] = values

        rows = pl.ds(pl.multiple_of((slot_zh * 4 + slot_y) * BLOCK, BLOCK), BLOCK)
        pltpu.make_async_copy(staged.at[k], out.at[rows], outs.at[k]).start()
        return carry

    lax.fori_loop(0, 8, unpack, 0)
    for k in range(8):
        pltpu.make_async_copy(staged.at[k], out.at[pl.ds(0, BLOCK)], outs.at[k]).wait()
    for c in started:
        c.wait_send()
    for condition, waits in ends:

        @pl.when(condition)
        def _():
            for w in waits:
                w()


def shards(slabs):
    flat = slabs.reshape(-1, BLOCK)
    blocks = flat.T.reshape(2, HALF, DEPTH)
    anywhere = pl.BlockSpec(memory_space=pl.ANY)
    dma = pltpu.SemaphoreType.DMA
    copies = 43
    return pl.pallas_call(
        kernel,
        out_shape=jax.ShapeDtypeStruct((8 * BLOCK, BLOCK), jnp.float32),
        in_specs=[anywhere],
        out_specs=anywhere,
        scratch_shapes=[
            pltpu.VMEM((4, 2, 2, HALF, DEPTH), jnp.bfloat16),
            pltpu.VMEM((4, 2, 2, HALF, DEPTH), jnp.bfloat16),
            pltpu.VMEM((16, BLOCK, BLOCK), jnp.float32),
            pltpu.VMEM((8, BLOCK, BLOCK), jnp.float32),
            pltpu.VMEM((8, 2, HALF, BLOCK), jnp.bfloat16),
            pltpu.VMEM((8, 2, 8, BLOCK), jnp.float32),
            pltpu.VMEM((2, 4, 2, HALF, BLOCK), jnp.bfloat16),
            pltpu.VMEM((2, 4, 2, 8, BLOCK), jnp.float32),
            pltpu.VMEM((8, BLOCK, BLOCK), jnp.float32),
            dma((copies,)), dma((copies,)), dma((3,)),
            dma((16,)), dma((8,)), dma((32,)), dma((16,)), dma((32,)), dma((16,)), dma((2,)), dma((8,)),
        ],
        compiler_params=pltpu.CompilerParams(collective_id=0, has_side_effects=True, vmem_limit_bytes=44 * 2**20),
        cost_estimate=pl.CostEstimate(flops=2 * 1536 * 1536 * 2048, bytes_accessed=4 * 2**20, transcendentals=0),
    )(blocks)


def solution(mesh):
    placed = (P("aux", None, "bas"),)
    return jax.shard_map(
        shards, mesh=mesh, in_specs=placed, out_specs=P("aux", "bas"), check_vma=False
    )
```

```python
import jax
import jax.numpy as jnp
from jax import lax
from jax.experimental import pallas as pl
from jax.experimental.pallas import tpu as pltpu
from jax.sharding import PartitionSpec as P

MESH = pl.DeviceIdType.MESH
BLOCK, HALF, QUARTER, DEPTH = 384, 192, 128, 1024
TOP = 208.0


def encode(tile):
    largest = jnp.max(jnp.abs(tile), axis=1, keepdims=True)
    largest = jnp.maximum(largest, 1e-30)
    t = tile * (TOP / largest)
    t2 = t * t
    t4 = t2 * t2
    code = (t4 * t4) * (t4 * t2) * (t * jnp.abs(t))
    return code.astype(jnp.bfloat16), largest * (1.0 / TOP)


def decode(code, factor):
    code = code.astype(jnp.float32)
    root = jnp.exp2(jnp.log2(jnp.abs(code)) * (1.0 / 16.0))
    return jnp.where(code < 0, -root, root) * factor


def place():
    aux, bas = lax.axis_index("aux"), lax.axis_index("bas")
    return aux // 2, lax.rem(aux, 2), bas // 8, lax.rem(bas // 4, 2), lax.rem(bas, 4)


def ring(v, step):
    return lax.rem(v + step + 4, 4)


def is_turned(dx, dy, across):
    far_x, far_y = min(dx, 4 - dx), min(dy, 4 - dy)
    if across:
        return (far_y == 1 and far_x != 1) or far_x == far_y == 2
    return far_y > 0


def kernel(block, out, bt, cb, rb, part, precv, enc, fac, land, factors, staged, ss, rs, ls, pss, prs, rss, rrs, fss, frs, os, outs):
    zl, h, x, zh, y = place()
    a = zl * 2 + h
    zb = lax.rem(zl + zh, 2)
    other = 1 - zb

    def device(x=x, y=y, zh=zh, zl=zl, h=h):
        return (zl * 2 + h, x * 8 + zh * 4 + y)

    right, left = {"y": ring(y, 1)}, {"y": ring(y, -1)}
    front, back = {"x": ring(x, 1)}, {"x": ring(x, -1)}
    a_dev = device(zl=1 - zl)
    b_dev = device(zl=1 - zl, zh=1 - zh)
    core_dev = device(h=1 - h)

    barrier = pltpu.get_barrier_semaphore()
    greeted = [device(**front), device(**back), b_dev, core_dev, a_dev]
    greeted += [device(y=ring(y, step), zl=z) for step in (1, 2, 3) for z in (zl, 1 - zl)]
    for d in greeted:
        pl.semaphore_signal(barrier, 1, device_id=d, device_id_type=MESH)
    alone = a == x
    for zh1 in range(2):
        for zl1 in range(2):
            same = jnp.logical_and(alone, jnp.logical_and(zh == zh1, zl == zl1))

            @pl.when(jnp.logical_not(same))
            def _():
                pl.semaphore_signal(barrier, 1, device_id=device(x=a, zh=zh1, zl=zl1, h=lax.rem(x, 2)), device_id_type=MESH)

    bt[...] = block[...].T.reshape(2, HALF, DEPTH)
    pl.semaphore_wait(barrier, len(greeted) + 4 - alone.astype(jnp.int32))

    started = []

    def send(src, dst, to):
        n = len(started)
        copy = pltpu.make_async_remote_copy(src, dst, ss.at[n], rs.at[n], device_id=to, device_id_type=MESH)
        copy.start()
        started.append(copy)
        return copy

    def local(src, dst, n):
        copy = pltpu.make_async_copy(src, dst, ls.at[n])
        copy.start()
        return copy

    def both(src, dst, plus, minus):
        return [send(src, dst, device(**plus)), send(src, dst, device(**minus))]

    def forward(slots, where, plus, minus, rows=HALF):
        lo, hi = pl.ds(0, rows // 2), pl.ds(rows // 2, rows // 2)
        one = slots(ring(where, -1)).at[lo]
        two = slots(ring(where, 1)).at[hi]
        return [send(one, one, device(**plus)), send(two, two, device(**minus))]

    def n1_slot(v):
        return cb.at[v, zl, zb]

    def n0_slot(v):
        return cb.at[v, zl, other]

    def p0_slot(v):
        return cb.at[v, 1 - zl, zb]

    def p1_slot(v):
        return cb.at[v, 1 - zl, other, pl.ds(0, QUARTER)]

    def a2_slot(v):
        return cb.at[v, zl, zb, pl.ds(QUARTER, HALF - QUARTER)]

    def q0_slot(v):
        return rb.at[v, zl, zh]

    def q1_slot(v):
        return rb.at[v, 1 - zl, 1 - zh]

    def q2_slot(v):
        return rb.at[v, 1 - zl, zh]

    def arrive(*copies):
        for group in copies:
            for c in group:
                c.wait_recv()

    def product(xs, ys):
        total = None
        for k in range(2):
            term = lax.dot_general(
                rb[xs, k].reshape(BLOCK, DEPTH), cb[ys, k].reshape(BLOCK, DEPTH), (((1,), (1,)), ((), ())), preferred_element_type=jnp.float32
            )
            total = term if total is None else total + term
        return total

    tasks, ends, pending, lag = [], [], [], 2

    def task(dx, dy):
        j = len(tasks)
        xs = ring(x, dx)
        keep = lax.rem(xs, 2) == h
        ys = ring(y, dy)
        spot = (xs // 2) * 4 + ys
        part[j] = product(xs, ys)
        copy = pltpu.make_async_remote_copy(part.at[j], precv.at[spot], pss.at[j], prs.at[spot], device_id=core_dev, device_id_type=MESH)
        pl.when(jnp.logical_not(keep))(copy.start)
        ends.append((jnp.logical_not(keep), [copy.wait_send]))
        tasks.append((dx, dy, xs, ys, keep, spot, copy))
        pending.append(j)
        if len(pending) > lag:
            finish(pending.pop(0))

    def flush():
        while pending:
            finish(pending.pop(0))

    def finish(j):
        dx, dy, xs, ys, keep, spot, exchanged = tasks[j]

        def deliver(zh1, owner, slot_zh, slot_y, mine):
            n = j * 2 + zh1
            piece = (slot_zh * 4 + slot_y) * 2 + zb
            src, src_factor = enc.at[spot, zh1], fac.at[spot, zh1]
            dst, dst_factor = land.at[slot_zh, slot_y, zb], factors.at[slot_zh, slot_y, zb]
            away = [
                pltpu.make_async_remote_copy(src, dst, rss.at[n], rrs.at[piece], device_id=owner, device_id_type=MESH),
                pltpu.make_async_remote_copy(src_factor, dst_factor, fss.at[n], frs.at[piece], device_id=owner, device_id_type=MESH),
            ]
            home = []
            if mine is not None:
                home = [pltpu.make_async_copy(src, dst, os.at[0]), pltpu.make_async_copy(src_factor, dst_factor, os.at[1])]
            ends.append((keep if mine is None else jnp.logical_and(keep, jnp.logical_not(mine)), [c.wait_send for c in away]))
            return away, home, mine

        pieces = []
        for across in (0, 1):
            zh1 = 1 - zh if across else zh
            if is_turned(dx, dy, across):
                mine = alone if dx == 0 and not across else None
                pieces.append(deliver(zh1, device(x=xs, zh=zh1, zl=x // 2, h=lax.rem(x, 2)), zh, ys, mine))
            else:
                mine = xs == a if dy == 0 else None
                pieces.append(deliver(zh1, device(y=ys, zl=xs // 2), zh1, y, mine))

        @pl.when(keep)
        def _():
            exchanged.wait_recv()
            code, factor = encode((part[j] + precv[spot]).reshape(2, HALF, BLOCK))
            enc[spot] = code
            fac[spot] = jnp.broadcast_to(factor, (2, 8, BLOCK))
            for away, home, mine in pieces:
                if mine is None:
                    for c in away:
                        c.start()
                    continue

                @pl.when(jnp.logical_not(mine))
                def _():
                    for c in away:
                        c.start()

                @pl.when(mine)
                def _():
                    for c in home:
                        c.start()
                    for c in home:
                        c.wait()

    a1 = [send(bt.at[other], cb.at[y, zl, other], a_dev)]
    b1 = [send(bt.at[zb], rb.at[x, zl, zh], b_dev)]
    n1 = both(bt.at[zb], cb.at[y, zl, zb], right, left)
    q0 = both(bt.at[zb], rb.at[x, zl, zh], front, back)
    a1b = [send(bt.at[zb, pl.ds(0, QUARTER)], cb.at[y, zl, zb, pl.ds(0, QUARTER)], a_dev)]
    a2 = {0: [send(bt.at[zb, pl.ds(QUARTER, HALF - QUARTER)], a2_slot(y), a_dev)]}
    b2 = {}
    l0 = local(bt, cb.at[y, zl], 0)
    l1 = local(bt.at[zb], rb.at[x, zl, zh], 1)

    arrive(a1)
    l2 = local(p0_slot(y), q2_slot(x), 2)
    q2 = both(p0_slot(y), q2_slot(x), front, back)
    p0 = both(p0_slot(y), p0_slot(y), right, left)
    b2[0] = [send(p0_slot(y), q2_slot(x), b_dev)]
    arrive(b1)
    q1 = both(q1_slot(x), q1_slot(x), front, back)
    n0 = both(bt.at[other], n0_slot(y), right, left)
    arrive(n1)
    for step in (3, 1):
        a2[step] = [send(a2_slot(ring(y, step)), a2_slot(ring(y, step)), a_dev)]
    arrive(a1b)
    p1 = both(p1_slot(y), p1_slot(y), right, left)
    l0.wait()
    l1.wait()
    l2.wait()
    arrive(q0, q2)
    for step in (3, 1):
        b2[step] = [send(q2_slot(ring(x, step)), q2_slot(ring(x, step)), b_dev)]
    q2f = forward(q2_slot, x, front, back)
    arrive(a2[0], b2[0])
    task(0, 0)
    arrive(p0)
    n1f = forward(n1_slot, y, right, left)
    arrive(q1)
    q0f = forward(q0_slot, x, front, back)
    q1f = forward(q1_slot, x, front, back)
    arrive(b2[3])
    task(3, 0)
    arrive(q2f)
    b2[2] = [send(q2_slot(ring(x, 2)), q2_slot(ring(x, 2)), b_dev)]
    arrive(n0)
    p0f = forward(p0_slot, y, right, left)
    n0f = forward(n0_slot, y, right, left)
    arrive(p1)
    p1f = forward(p1_slot, y, right, left, QUARTER)
    arrive(a2[3], a2[1])
    task(0, 3)
    task(0, 1)
    arrive(n1f)
    a2[2] = [send(a2_slot(ring(y, 2)), a2_slot(ring(y, 2)), a_dev)]
    task(3, 3)
    task(3, 1)
    arrive(b2[1])
    task(1, 0)
    task(1, 3)
    task(1, 1)
    arrive(q0f, q1f, b2[2])
    task(2, 0)
    task(2, 3)
    task(2, 1)
    arrive(p0f, n0f, p1f, a2[2])
    task(2, 2)
    task(3, 2)
    task(1, 2)
    task(0, 2)
    flush()

    def unpack(k, carry):
        q = k // 2
        slot_zh = lax.rem(k, 2)
        step = q + (q == 2).astype(jnp.int32) - (q == 3).astype(jnp.int32)
        slot_y = ring(y, step)
        for slot_zb in range(2):
            mine = jnp.logical_and(slot_zb == zb, jnp.logical_or(step == 0, jnp.logical_and(alone, slot_zh == zh)))
            piece = (slot_zh * 4 + slot_y) * 2 + slot_zb

            @pl.when(jnp.logical_not(mine))
            def _():
                dst, dst_factor = land.at[slot_zh, slot_y, slot_zb], factors.at[slot_zh, slot_y, slot_zb]
                pltpu.make_async_remote_copy(enc.at[0, 0], dst, rss.at[0], rrs.at[piece], device_id=a_dev, device_id_type=MESH).wait_recv()
                pltpu.make_async_remote_copy(fac.at[0, 0], dst_factor, fss.at[0], frs.at[piece], device_id=a_dev, device_id_type=MESH).wait_recv()

        values = decode(land[slot_zh, slot_y], factors[slot_zh, slot_y, :, :1]).reshape(BLOCK, BLOCK)
        dx, dy = ring(a, -x), lax.rem(4 - step, 4)
        far_x, far_y = jnp.minimum(dx, 4 - dx), jnp.minimum(dy, 4 - dy)
        both_far = jnp.logical_and(far_x == 2, far_y == 2)
        spread = jnp.logical_or(jnp.logical_and(far_y == 1, far_x != 1), both_far)
        turned = jnp.where(slot_zh == zh, far_y > 0, spread)

        @pl.when(turned)
        def _():
            staged[k] = values.T

        @pl.when(jnp.logical_not(turned))
        def _():
            staged[k] = values

        rows = pl.ds(pl.multiple_of((slot_zh * 4 + slot_y) * BLOCK, BLOCK), BLOCK)
        pltpu.make_async_copy(staged.at[k], out.at[rows], outs.at[k]).start()
        return carry

    lax.fori_loop(0, 8, unpack, 0)
    for k in range(8):
        pltpu.make_async_copy(staged.at[k], out.at[pl.ds(0, BLOCK)], outs.at[k]).wait()
    for c in started:
        c.wait_send()
    for condition, waits in ends:

        @pl.when(condition)
        def _():
            for w in waits:
                w()


def shards(slabs):
    flat = slabs.reshape(-1, BLOCK)
    anywhere = pl.BlockSpec(memory_space=pl.ANY)
    dma = pltpu.SemaphoreType.DMA
    copies = 43
    return pl.pallas_call(
        kernel,
        out_shape=jax.ShapeDtypeStruct((8 * BLOCK, BLOCK), jnp.float32),
        in_specs=[pl.BlockSpec(memory_space=pltpu.VMEM)],
        out_specs=anywhere,
        scratch_shapes=[
            pltpu.VMEM((2, HALF, DEPTH), jnp.bfloat16),
            pltpu.VMEM((4, 2, 2, HALF, DEPTH), jnp.bfloat16),
            pltpu.VMEM((4, 2, 2, HALF, DEPTH), jnp.bfloat16),
            pltpu.VMEM((16, BLOCK, BLOCK), jnp.float32),
            pltpu.VMEM((8, BLOCK, BLOCK), jnp.float32),
            pltpu.VMEM((8, 2, HALF, BLOCK), jnp.bfloat16),
            pltpu.VMEM((8, 2, 8, BLOCK), jnp.float32),
            pltpu.VMEM((2, 4, 2, HALF, BLOCK), jnp.bfloat16),
            pltpu.VMEM((2, 4, 2, 8, BLOCK), jnp.float32),
            pltpu.VMEM((8, BLOCK, BLOCK), jnp.float32),
            dma((copies,)), dma((copies,)), dma((3,)),
            dma((16,)), dma((8,)), dma((32,)), dma((16,)), dma((32,)), dma((16,)), dma((2,)), dma((8,)),
        ],
        compiler_params=pltpu.CompilerParams(collective_id=0, has_side_effects=True, vmem_limit_bytes=44 * 2**20),
        cost_estimate=pl.CostEstimate(flops=2 * 1536 * 1536 * 2048, bytes_accessed=4 * 2**20, transcendentals=0),
    )(flat)


def solution(mesh):
    placed = (P("aux", None, "bas"),)
    return jax.shard_map(
        shards, mesh=mesh, in_specs=placed, out_specs=P("aux", "bas"), check_vma=False
    )
```

```python
import jax
import jax.numpy as jnp
from jax import lax
from jax.experimental import pallas as pl
from jax.experimental.pallas import tpu as pltpu
from jax.sharding import PartitionSpec as P

MESH = pl.DeviceIdType.MESH
BLOCK, HALF, QUARTER, DEPTH = 384, 192, 128, 1024
ROWS = 208
TOP = 208.0


def encode(tile):
    largest = jnp.max(jnp.abs(tile), axis=1, keepdims=True)
    factor = (jnp.maximum(largest, 1e-30) * (1.0 / TOP)).astype(jnp.bfloat16)
    t = tile * (1.0 / factor.astype(jnp.float32))
    t2 = t * t
    t4 = t2 * t2
    code = (t4 * t4) * (t4 * t2) * (t * jnp.abs(t))
    return code.astype(jnp.bfloat16), jnp.broadcast_to(factor, (2, ROWS - HALF, BLOCK))


def decode(piece):
    code = piece[:, :HALF].astype(jnp.float32)
    root = jnp.exp2(jnp.log2(jnp.abs(code)) * (1.0 / 16.0))
    return jnp.where(code < 0, -root, root) * piece[:, HALF : HALF + 1].astype(jnp.float32)


def place():
    aux, bas = lax.axis_index("aux"), lax.axis_index("bas")
    return aux // 2, lax.rem(aux, 2), bas // 8, lax.rem(bas // 4, 2), lax.rem(bas, 4)


def ring(v, step):
    return lax.rem(v + step + 4, 4)


def is_turned(dx, dy, across):
    far_x, far_y = min(dx, 4 - dx), min(dy, 4 - dy)
    if across:
        return (far_y == 1 and far_x != 1) or far_x == far_y == 2
    return far_y > 0


def kernel(block, out, bt, cb, rb, part, precv, enc, land, staged, ss, rs, ls, pss, prs, rss, rrs, os, outs):
    zl, h, x, zh, y = place()
    a = zl * 2 + h
    zb = lax.rem(zl + zh, 2)
    other = 1 - zb

    def device(x=x, y=y, zh=zh, zl=zl, h=h):
        return (zl * 2 + h, x * 8 + zh * 4 + y)

    right, left = {"y": ring(y, 1)}, {"y": ring(y, -1)}
    front, back = {"x": ring(x, 1)}, {"x": ring(x, -1)}
    a_dev = device(zl=1 - zl)
    b_dev = device(zl=1 - zl, zh=1 - zh)
    core_dev = device(h=1 - h)

    barrier = pltpu.get_barrier_semaphore()
    greeted = [device(**front), device(**back), b_dev, core_dev, a_dev]
    greeted += [device(y=ring(y, step), zl=z) for step in (1, 2, 3) for z in (zl, 1 - zl)]
    for d in greeted:
        pl.semaphore_signal(barrier, 1, device_id=d, device_id_type=MESH)
    alone = a == x
    for zh1 in range(2):
        for zl1 in range(2):
            same = jnp.logical_and(alone, jnp.logical_and(zh == zh1, zl == zl1))

            @pl.when(jnp.logical_not(same))
            def _():
                pl.semaphore_signal(barrier, 1, device_id=device(x=a, zh=zh1, zl=zl1, h=lax.rem(x, 2)), device_id_type=MESH)

    bt[...] = block[...].T.reshape(2, HALF, DEPTH)
    pl.semaphore_wait(barrier, len(greeted) + 4 - alone.astype(jnp.int32))

    started = []

    def send(src, dst, to):
        n = len(started)
        copy = pltpu.make_async_remote_copy(src, dst, ss.at[n], rs.at[n], device_id=to, device_id_type=MESH)
        copy.start()
        started.append(copy)
        return copy

    def local(src, dst, n):
        copy = pltpu.make_async_copy(src, dst, ls.at[n])
        copy.start()
        return copy

    def both(src, dst, plus, minus):
        return [send(src, dst, device(**plus)), send(src, dst, device(**minus))]

    def forward(slots, where, plus, minus, rows=HALF):
        lo, hi = pl.ds(0, rows // 2), pl.ds(rows // 2, rows // 2)
        one = slots(ring(where, -1)).at[lo]
        two = slots(ring(where, 1)).at[hi]
        return [send(one, one, device(**plus)), send(two, two, device(**minus))]

    def n1_slot(v):
        return cb.at[v, zl, zb]

    def n0_slot(v):
        return cb.at[v, zl, other]

    def p0_slot(v):
        return cb.at[v, 1 - zl, zb]

    def p1_slot(v):
        return cb.at[v, 1 - zl, other, pl.ds(0, QUARTER)]

    def a2_slot(v):
        return cb.at[v, zl, zb, pl.ds(QUARTER, HALF - QUARTER)]

    def q0_slot(v):
        return rb.at[v, zl, zh]

    def q1_slot(v):
        return rb.at[v, 1 - zl, 1 - zh]

    def q2_slot(v):
        return rb.at[v, 1 - zl, zh]

    def arrive(*copies):
        for group in copies:
            for c in group:
                c.wait_recv()

    def product(xs, ys):
        total = None
        for k in range(2):
            term = lax.dot_general(
                rb[xs, k].reshape(BLOCK, DEPTH), cb[ys, k].reshape(BLOCK, DEPTH), (((1,), (1,)), ((), ())), preferred_element_type=jnp.float32
            )
            total = term if total is None else total + term
        return total

    tasks, ends, pending, lag = [], [], [], 1

    def task(dx, dy):
        j = len(tasks)
        xs = ring(x, dx)
        keep = lax.rem(xs, 2) == h
        ys = ring(y, dy)
        spot = (xs // 2) * 4 + ys
        part[j] = product(xs, ys)
        copy = pltpu.make_async_remote_copy(part.at[j], precv.at[spot], pss.at[j], prs.at[spot], device_id=core_dev, device_id_type=MESH)
        pl.when(jnp.logical_not(keep))(copy.start)
        ends.append((jnp.logical_not(keep), [copy.wait_send]))
        tasks.append((dx, dy, xs, ys, keep, spot, copy))
        pending.append(j)
        if len(pending) > lag:
            finish(pending.pop(0))

    def flush():
        while pending:
            finish(pending.pop(0))

    def finish(j):
        dx, dy, xs, ys, keep, spot, exchanged = tasks[j]

        def deliver(zh1, owner, slot_zh, slot_y, mine):
            n = j * 2 + zh1
            piece = (slot_zh * 4 + slot_y) * 2 + zb
            src, dst = enc.at[spot, zh1], land.at[slot_zh, slot_y, zb]
            away = [
                pltpu.make_async_remote_copy(src, dst, rss.at[n], rrs.at[piece], device_id=owner, device_id_type=MESH),
            ]
            home = []
            if mine is not None:
                home = [pltpu.make_async_copy(src, dst, os.at[0])]
            ends.append((keep if mine is None else jnp.logical_and(keep, jnp.logical_not(mine)), [c.wait_send for c in away]))
            return away, home, mine

        pieces = []
        for across in (0, 1):
            zh1 = 1 - zh if across else zh
            if is_turned(dx, dy, across):
                mine = alone if dx == 0 and not across else None
                pieces.append(deliver(zh1, device(x=xs, zh=zh1, zl=x // 2, h=lax.rem(x, 2)), zh, ys, mine))
            else:
                mine = xs == a if dy == 0 else None
                pieces.append(deliver(zh1, device(y=ys, zl=xs // 2), zh1, y, mine))

        @pl.when(keep)
        def _():
            exchanged.wait_recv()
            code, factor = encode((part[j] + precv[spot]).reshape(2, HALF, BLOCK))
            enc[spot, :, :HALF] = code
            enc[spot, :, HALF:] = factor
            for away, home, mine in pieces:
                if mine is None:
                    for c in away:
                        c.start()
                    continue

                @pl.when(jnp.logical_not(mine))
                def _():
                    for c in away:
                        c.start()

                @pl.when(mine)
                def _():
                    for c in home:
                        c.start()
                    for c in home:
                        c.wait()

    a1 = [send(bt.at[other], cb.at[y, zl, other], a_dev)]
    b1 = [send(bt.at[zb], rb.at[x, zl, zh], b_dev)]
    n1 = both(bt.at[zb], cb.at[y, zl, zb], right, left)
    q0 = both(bt.at[zb], rb.at[x, zl, zh], front, back)
    a1b = [send(bt.at[zb, pl.ds(0, QUARTER)], cb.at[y, zl, zb, pl.ds(0, QUARTER)], a_dev)]
    a2 = {0: [send(bt.at[zb, pl.ds(QUARTER, HALF - QUARTER)], a2_slot(y), a_dev)]}
    b2 = {}
    l0 = local(bt, cb.at[y, zl], 0)
    l1 = local(bt.at[zb], rb.at[x, zl, zh], 1)

    arrive(a1)
    l2 = local(p0_slot(y), q2_slot(x), 2)
    q2 = both(p0_slot(y), q2_slot(x), front, back)
    p0 = both(p0_slot(y), p0_slot(y), right, left)
    b2[0] = [send(p0_slot(y), q2_slot(x), b_dev)]
    arrive(b1)
    q1 = both(q1_slot(x), q1_slot(x), front, back)
    n0 = both(bt.at[other], n0_slot(y), right, left)
    arrive(n1)
    for step in (3, 1):
        a2[step] = [send(a2_slot(ring(y, step)), a2_slot(ring(y, step)), a_dev)]
    arrive(a1b)
    p1 = both(p1_slot(y), p1_slot(y), right, left)
    l0.wait()
    l1.wait()
    l2.wait()
    arrive(q0, q2)
    for step in (3, 1):
        b2[step] = [send(q2_slot(ring(x, step)), q2_slot(ring(x, step)), b_dev)]
    q2f = forward(q2_slot, x, front, back)
    arrive(a2[0], b2[0])
    task(0, 0)
    arrive(p0)
    n1f = forward(n1_slot, y, right, left)
    arrive(q1)
    q0f = forward(q0_slot, x, front, back)
    q1f = forward(q1_slot, x, front, back)
    arrive(b2[3])
    task(3, 0)
    arrive(q2f)
    b2[2] = [send(q2_slot(ring(x, 2)), q2_slot(ring(x, 2)), b_dev)]
    arrive(n0)
    p0f = forward(p0_slot, y, right, left)
    n0f = forward(n0_slot, y, right, left)
    arrive(p1)
    p1f = forward(p1_slot, y, right, left, QUARTER)
    arrive(a2[3], a2[1])
    task(0, 3)
    task(0, 1)
    arrive(n1f)
    a2[2] = [send(a2_slot(ring(y, 2)), a2_slot(ring(y, 2)), a_dev)]
    task(3, 3)
    task(3, 1)
    arrive(b2[1])
    task(1, 0)
    task(1, 3)
    task(1, 1)
    arrive(q0f, q1f, b2[2])
    task(2, 0)
    task(2, 3)
    task(2, 1)
    arrive(p0f, n0f, p1f, a2[2])
    task(2, 2)
    task(3, 2)
    task(1, 2)
    task(0, 2)
    flush()

    def unpack(k, carry):
        q = k // 2
        slot_zh = lax.rem(k, 2)
        step = q + (q == 2).astype(jnp.int32) - (q == 3).astype(jnp.int32)
        slot_y = ring(y, step)
        for slot_zb in range(2):
            mine = jnp.logical_and(slot_zb == zb, jnp.logical_or(step == 0, jnp.logical_and(alone, slot_zh == zh)))
            piece = (slot_zh * 4 + slot_y) * 2 + slot_zb

            @pl.when(jnp.logical_not(mine))
            def _():
                dst = land.at[slot_zh, slot_y, slot_zb]
                pltpu.make_async_remote_copy(enc.at[0, 0], dst, rss.at[0], rrs.at[piece], device_id=a_dev, device_id_type=MESH).wait_recv()

        values = decode(land[slot_zh, slot_y]).reshape(BLOCK, BLOCK)
        dx, dy = ring(a, -x), lax.rem(4 - step, 4)
        far_x, far_y = jnp.minimum(dx, 4 - dx), jnp.minimum(dy, 4 - dy)
        both_far = jnp.logical_and(far_x == 2, far_y == 2)
        spread = jnp.logical_or(jnp.logical_and(far_y == 1, far_x != 1), both_far)
        turned = jnp.where(slot_zh == zh, far_y > 0, spread)

        @pl.when(turned)
        def _():
            staged[k] = values.T

        @pl.when(jnp.logical_not(turned))
        def _():
            staged[k] = values

        rows = pl.ds(pl.multiple_of((slot_zh * 4 + slot_y) * BLOCK, BLOCK), BLOCK)
        pltpu.make_async_copy(staged.at[k], out.at[rows], outs.at[k]).start()
        return carry

    lax.fori_loop(0, 8, unpack, 0)
    for k in range(8):
        pltpu.make_async_copy(staged.at[k], out.at[pl.ds(0, BLOCK)], outs.at[k]).wait()
    for c in started:
        c.wait_send()
    for condition, waits in ends:

        @pl.when(condition)
        def _():
            for w in waits:
                w()


def shards(slabs):
    flat = slabs.reshape(-1, BLOCK)
    anywhere = pl.BlockSpec(memory_space=pl.ANY)
    dma = pltpu.SemaphoreType.DMA
    copies = 43
    return pl.pallas_call(
        kernel,
        out_shape=jax.ShapeDtypeStruct((8 * BLOCK, BLOCK), jnp.float32),
        in_specs=[pl.BlockSpec(memory_space=pltpu.VMEM)],
        out_specs=anywhere,
        scratch_shapes=[
            pltpu.VMEM((2, HALF, DEPTH), jnp.bfloat16),
            pltpu.VMEM((4, 2, 2, HALF, DEPTH), jnp.bfloat16),
            pltpu.VMEM((4, 2, 2, HALF, DEPTH), jnp.bfloat16),
            pltpu.VMEM((16, BLOCK, BLOCK), jnp.float32),
            pltpu.VMEM((8, BLOCK, BLOCK), jnp.float32),
            pltpu.VMEM((8, 2, ROWS, BLOCK), jnp.bfloat16),
            pltpu.VMEM((2, 4, 2, ROWS, BLOCK), jnp.bfloat16),
            pltpu.VMEM((8, BLOCK, BLOCK), jnp.float32),
            dma((copies,)), dma((copies,)), dma((3,)),
            dma((16,)), dma((8,)), dma((32,)), dma((16,)), dma((2,)), dma((8,)),
        ],
        compiler_params=pltpu.CompilerParams(collective_id=0, has_side_effects=True, vmem_limit_bytes=44 * 2**20),
        cost_estimate=pl.CostEstimate(flops=2 * 1536 * 1536 * 2048, bytes_accessed=4 * 2**20, transcendentals=0),
    )(flat)


def solution(mesh):
    placed = (P("aux", None, "bas"),)
    return jax.shard_map(
        shards, mesh=mesh, in_specs=placed, out_specs=P("aux", "bas"), check_vma=False
    )
```

```python
import jax
import jax.numpy as jnp
from jax import lax
from jax.experimental import pallas as pl
from jax.experimental.pallas import tpu as pltpu
from jax.sharding import PartitionSpec as P

MESH = pl.DeviceIdType.MESH
BLOCK, HALF, QUARTER, DEPTH = 384, 192, 128, 1024
ROWS = 208
TOP = 208.0


def encode(tile):
    largest = jnp.max(jnp.abs(tile), axis=1, keepdims=True)
    factor = (jnp.maximum(largest, 1e-30) * (1.0 / TOP)).astype(jnp.bfloat16)
    t = tile * (1.0 / factor.astype(jnp.float32))
    t2 = t * t
    t4 = t2 * t2
    code = (t4 * t4) * (t4 * t2) * (t * jnp.abs(t))
    return code.astype(jnp.bfloat16), jnp.broadcast_to(factor, (2, ROWS - HALF, BLOCK))


def decode(piece):
    code = piece[:, :HALF].astype(jnp.float32)
    root = jnp.exp2(jnp.log2(jnp.abs(code)) * (1.0 / 16.0))
    return jnp.where(code < 0, -root, root) * piece[:, HALF : HALF + 1].astype(jnp.float32)


def place():
    aux, bas = lax.axis_index("aux"), lax.axis_index("bas")
    return aux // 2, lax.rem(aux, 2), bas // 8, lax.rem(bas // 4, 2), lax.rem(bas, 4)


def ring(v, step):
    return lax.rem(v + step + 4, 4)


def is_turned(dx, dy, across):
    far_x, far_y = min(dx, 4 - dx), min(dy, 4 - dy)
    if across:
        return (far_y == 1 and far_x != 1) or far_x == far_y == 2
    return far_y > 0


def kernel(block, out, bt, cb, rb, part, precv, enc, land, staged, ss, rs, ls, pss, prs, rss, rrs, os, outs):
    zl, h, x, zh, y = place()
    a = zl * 2 + h
    zb = lax.rem(zl + zh, 2)
    other = 1 - zb

    def device(x=x, y=y, zh=zh, zl=zl, h=h):
        return (zl * 2 + h, x * 8 + zh * 4 + y)

    right, left = {"y": ring(y, 1)}, {"y": ring(y, -1)}
    front, back = {"x": ring(x, 1)}, {"x": ring(x, -1)}
    a_dev = device(zl=1 - zl)
    b_dev = device(zl=1 - zl, zh=1 - zh)
    core_dev = device(h=1 - h)

    barrier = pltpu.get_barrier_semaphore()
    greeted = [device(**front), device(**back), b_dev, core_dev, a_dev]
    greeted += [device(y=ring(y, step), zl=z) for step in (1, 2, 3) for z in (zl, 1 - zl)]
    for d in greeted:
        pl.semaphore_signal(barrier, 1, device_id=d, device_id_type=MESH)
    alone = a == x
    for zh1 in range(2):
        for zl1 in range(2):
            same = jnp.logical_and(alone, jnp.logical_and(zh == zh1, zl == zl1))

            @pl.when(jnp.logical_not(same))
            def _():
                pl.semaphore_signal(barrier, 1, device_id=device(x=a, zh=zh1, zl=zl1, h=lax.rem(x, 2)), device_id_type=MESH)

    bt[...] = block[...].T.reshape(2, HALF, DEPTH)
    pl.semaphore_wait(barrier, len(greeted) + 4 - alone.astype(jnp.int32))

    started = []

    def send(src, dst, to):
        n = len(started)
        copy = pltpu.make_async_remote_copy(src, dst, ss.at[n], rs.at[n], device_id=to, device_id_type=MESH)
        copy.start()
        started.append(copy)
        return copy

    def local(src, dst, n):
        copy = pltpu.make_async_copy(src, dst, ls.at[n])
        copy.start()
        return copy

    def both(src, dst, plus, minus):
        return [send(src, dst, device(**plus)), send(src, dst, device(**minus))]

    def forward(slots, where, plus, minus, rows=HALF):
        lo, hi = pl.ds(0, rows // 2), pl.ds(rows // 2, rows // 2)
        one = slots(ring(where, -1)).at[lo]
        two = slots(ring(where, 1)).at[hi]
        return [send(one, one, device(**plus)), send(two, two, device(**minus))]

    def n1_slot(v):
        return cb.at[v, zl, zb]

    def n0_slot(v):
        return cb.at[v, zl, other]

    def p0_slot(v):
        return cb.at[v, 1 - zl, zb]

    def p1_slot(v):
        return cb.at[v, 1 - zl, other, pl.ds(0, QUARTER)]

    def a2_slot(v):
        return cb.at[v, zl, zb, pl.ds(QUARTER, HALF - QUARTER)]

    def q0_slot(v):
        return rb.at[v, zl, zh]

    def q1_slot(v):
        return rb.at[v, 1 - zl, 1 - zh]

    def q2_slot(v):
        return rb.at[v, 1 - zl, zh]

    def arrive(*copies):
        for group in copies:
            for c in group:
                c.wait_recv()

    def product(xs, ys):
        total = None
        for k in range(2):
            term = lax.dot_general(
                rb[xs, k].reshape(BLOCK, DEPTH), cb[ys, k].reshape(BLOCK, DEPTH), (((1,), (1,)), ((), ())), preferred_element_type=jnp.float32
            )
            total = term if total is None else total + term
        return total

    tasks, ends, pending, lag = [], [], [], 1

    def task(dx, dy):
        j = len(tasks)
        xs = ring(x, dx)
        keep = lax.rem(xs, 2) == h
        ys = ring(y, dy)
        spot = (xs // 2) * 4 + ys
        part[j] = product(xs, ys)
        copy = pltpu.make_async_remote_copy(part.at[j], precv.at[spot], pss.at[j], prs.at[spot], device_id=core_dev, device_id_type=MESH)
        pl.when(jnp.logical_not(keep))(copy.start)
        ends.append((jnp.logical_not(keep), [copy.wait_send]))
        tasks.append((dx, dy, xs, ys, keep, spot, copy))
        pending.append(j)
        if len(pending) > lag:
            finish(pending.pop(0))

    def flush():
        while pending:
            finish(pending.pop(0))

    def finish(j):
        dx, dy, xs, ys, keep, spot, exchanged = tasks[j]

        def deliver(zh1, owner, slot_zh, slot_y, mine):
            n = j * 2 + zh1
            piece = (slot_zh * 4 + slot_y) * 2 + zb
            src, dst = enc.at[spot, zh1], land.at[slot_zh, slot_y, zb]
            away = [
                pltpu.make_async_remote_copy(src, dst, rss.at[n], rrs.at[piece], device_id=owner, device_id_type=MESH),
            ]
            home = []
            if mine is not None:
                home = [pltpu.make_async_copy(src, dst, os.at[0])]
            ends.append((keep if mine is None else jnp.logical_and(keep, jnp.logical_not(mine)), [c.wait_send for c in away]))
            return away, home, mine

        pieces = []
        for across in (0, 1):
            zh1 = 1 - zh if across else zh
            if is_turned(dx, dy, across):
                mine = alone if dx == 0 and not across else None
                pieces.append(deliver(zh1, device(x=xs, zh=zh1, zl=x // 2, h=lax.rem(x, 2)), zh, ys, mine))
            else:
                mine = xs == a if dy == 0 else None
                pieces.append(deliver(zh1, device(y=ys, zl=xs // 2), zh1, y, mine))

        @pl.when(keep)
        def _():
            exchanged.wait_recv()
            code, factor = encode((part[j] + precv[spot]).reshape(2, HALF, BLOCK))
            enc[spot, :, :HALF] = code
            enc[spot, :, HALF:] = factor
            for away, home, mine in pieces:
                if mine is None:
                    for c in away:
                        c.start()
                    continue

                @pl.when(jnp.logical_not(mine))
                def _():
                    for c in away:
                        c.start()

                @pl.when(mine)
                def _():
                    for c in home:
                        c.start()
                    for c in home:
                        c.wait()

    a1 = [send(bt.at[other], cb.at[y, zl, other], a_dev)]
    b1 = [send(bt.at[zb], rb.at[x, zl, zh], b_dev)]
    n1 = both(bt.at[zb], cb.at[y, zl, zb], right, left)
    q0 = both(bt.at[zb], rb.at[x, zl, zh], front, back)
    a1b = [send(bt.at[zb, pl.ds(0, QUARTER)], cb.at[y, zl, zb, pl.ds(0, QUARTER)], a_dev)]
    a2 = {0: [send(bt.at[zb, pl.ds(QUARTER, HALF - QUARTER)], a2_slot(y), a_dev)]}
    b2 = {}
    l0 = local(bt, cb.at[y, zl], 0)
    l1 = local(bt.at[zb], rb.at[x, zl, zh], 1)

    arrive(a1)
    l2 = local(p0_slot(y), q2_slot(x), 2)
    q2 = both(p0_slot(y), q2_slot(x), front, back)
    p0 = both(p0_slot(y), p0_slot(y), right, left)
    b2[0] = [send(p0_slot(y), q2_slot(x), b_dev)]
    arrive(b1)
    q1 = both(q1_slot(x), q1_slot(x), front, back)
    n0 = both(bt.at[other], n0_slot(y), right, left)
    arrive(n1)
    for step in (3, 1):
        a2[step] = [send(a2_slot(ring(y, step)), a2_slot(ring(y, step)), a_dev)]
    n1f = forward(n1_slot, y, right, left)
    arrive(a1b)
    p1 = both(p1_slot(y), p1_slot(y), right, left)
    l0.wait()
    l1.wait()
    l2.wait()
    arrive(q0, q2)
    for step in (3, 1):
        b2[step] = [send(q2_slot(ring(x, step)), q2_slot(ring(x, step)), b_dev)]
    q2f = forward(q2_slot, x, front, back)
    arrive(a2[0], b2[0])
    task(0, 0)
    arrive(p0)
    arrive(q1)
    q0f = forward(q0_slot, x, front, back)
    q1f = forward(q1_slot, x, front, back)
    arrive(b2[3])
    task(3, 0)
    arrive(q2f)
    b2[2] = [send(q2_slot(ring(x, 2)), q2_slot(ring(x, 2)), b_dev)]
    arrive(n0)
    p0f = forward(p0_slot, y, right, left)
    n0f = forward(n0_slot, y, right, left)
    arrive(p1)
    p1f = forward(p1_slot, y, right, left, QUARTER)
    arrive(a2[3], a2[1])
    task(0, 3)
    task(0, 1)
    arrive(n1f)
    a2[2] = [send(a2_slot(ring(y, 2)), a2_slot(ring(y, 2)), a_dev)]
    task(3, 3)
    task(3, 1)
    arrive(b2[1])
    task(1, 0)
    task(1, 3)
    task(1, 1)
    arrive(q0f, q1f, b2[2])
    task(2, 0)
    task(2, 3)
    task(2, 1)
    arrive(p0f, n0f, p1f, a2[2])
    task(2, 2)
    task(3, 2)
    task(1, 2)
    task(0, 2)
    flush()

    def unpack(k, carry):
        q = k // 2
        slot_zh = lax.rem(k, 2)
        step = q + (q == 2).astype(jnp.int32) - (q == 3).astype(jnp.int32)
        slot_y = ring(y, step)
        for slot_zb in range(2):
            mine = jnp.logical_and(slot_zb == zb, jnp.logical_or(step == 0, jnp.logical_and(alone, slot_zh == zh)))
            piece = (slot_zh * 4 + slot_y) * 2 + slot_zb

            @pl.when(jnp.logical_not(mine))
            def _():
                dst = land.at[slot_zh, slot_y, slot_zb]
                pltpu.make_async_remote_copy(enc.at[0, 0], dst, rss.at[0], rrs.at[piece], device_id=a_dev, device_id_type=MESH).wait_recv()

        values = decode(land[slot_zh, slot_y]).reshape(BLOCK, BLOCK)
        dx, dy = ring(a, -x), lax.rem(4 - step, 4)
        far_x, far_y = jnp.minimum(dx, 4 - dx), jnp.minimum(dy, 4 - dy)
        both_far = jnp.logical_and(far_x == 2, far_y == 2)
        spread = jnp.logical_or(jnp.logical_and(far_y == 1, far_x != 1), both_far)
        turned = jnp.where(slot_zh == zh, far_y > 0, spread)

        @pl.when(turned)
        def _():
            staged[k] = values.T

        @pl.when(jnp.logical_not(turned))
        def _():
            staged[k] = values

        rows = pl.ds(pl.multiple_of((slot_zh * 4 + slot_y) * BLOCK, BLOCK), BLOCK)
        pltpu.make_async_copy(staged.at[k], out.at[rows], outs.at[k]).start()
        return carry

    lax.fori_loop(0, 8, unpack, 0)
    for k in range(8):
        pltpu.make_async_copy(staged.at[k], out.at[pl.ds(0, BLOCK)], outs.at[k]).wait()
    for c in started:
        c.wait_send()
    for condition, waits in ends:

        @pl.when(condition)
        def _():
            for w in waits:
                w()


def shards(slabs):
    flat = slabs.reshape(-1, BLOCK)
    anywhere = pl.BlockSpec(memory_space=pl.ANY)
    dma = pltpu.SemaphoreType.DMA
    copies = 43
    return pl.pallas_call(
        kernel,
        out_shape=jax.ShapeDtypeStruct((8 * BLOCK, BLOCK), jnp.float32),
        in_specs=[pl.BlockSpec(memory_space=pltpu.VMEM)],
        out_specs=anywhere,
        scratch_shapes=[
            pltpu.VMEM((2, HALF, DEPTH), jnp.bfloat16),
            pltpu.VMEM((4, 2, 2, HALF, DEPTH), jnp.bfloat16),
            pltpu.VMEM((4, 2, 2, HALF, DEPTH), jnp.bfloat16),
            pltpu.VMEM((16, BLOCK, BLOCK), jnp.float32),
            pltpu.VMEM((8, BLOCK, BLOCK), jnp.float32),
            pltpu.VMEM((8, 2, ROWS, BLOCK), jnp.bfloat16),
            pltpu.VMEM((2, 4, 2, ROWS, BLOCK), jnp.bfloat16),
            pltpu.VMEM((8, BLOCK, BLOCK), jnp.float32),
            dma((copies,)), dma((copies,)), dma((3,)),
            dma((16,)), dma((8,)), dma((32,)), dma((16,)), dma((2,)), dma((8,)),
        ],
        compiler_params=pltpu.CompilerParams(collective_id=0, has_side_effects=True, vmem_limit_bytes=44 * 2**20),
        cost_estimate=pl.CostEstimate(flops=2 * 1536 * 1536 * 2048, bytes_accessed=4 * 2**20, transcendentals=0),
    )(flat)


def solution(mesh):
    placed = (P("aux", None, "bas"),)
    return jax.shard_map(
        shards, mesh=mesh, in_specs=placed, out_specs=P("aux", "bas"), check_vma=False
    )
```
